256 devices in a mesh: blk: 8 (over z_hi, core), head: 32 (over y, z_lo, x).
Axes of the slice: x: 4, y: 4, z: 8 (z_hi: 4, z_lo: 2; z = z_hi * 2 + z_lo), core: 2. Of those that a mesh axis runs over, the one named last changes fastest.
Arguments:
- tokens_qkv: bfloat16 [8192, 12288], P(('blk', 'head')), may hold values from -8 to 8, as said below
- block_mask: int32 [64, 64], replicated, may hold values from 0 to 1, as said below
Outputs:
- attended: bfloat16 [8192, 4096], P(('blk', 'head'))
The draws below stay inside these ranges and needn't reach their ends.
Inputs may be any that keep to these rules, and one draw needn't show every extreme that they name: `tokens_qkv`: queries, keys and values ordered by head, then query, key, value, then the 128 entries. `block_mask`: 1 where a pair of 128-token blocks attends; a block always attends to itself whatever the entry says.
All inputs are finite; a program needn't handle non-finite values.
Results may differ from the reference program's by a relative error of at most 0.007.
Values may be sent and summed in bfloat16 or wider, within the bound.
A program may use at most 64 MiB of HBM per device.

```python
import jax
import jax.numpy as jnp
from jax import lax

HEADS = 32
HD = 128
BLOCK = 128
SEQ_DEV = 1024
TOKENS = 8192
NB = 64


def draw_tokens_qkv(key, part):
    keys_list = jax.random.split(jax.random.fold_in(key, 11), 1)
    base = jnp.clip(jax.random.normal(keys_list[0], (TOKENS, HEADS, 3, HD), jnp.float32), -8.0, 8.0)
    return base.reshape(TOKENS, 3 * HEADS * HD).astype(jnp.bfloat16)


def draw_block_mask(key, part):
    first, second = jax.random.split(jax.random.fold_in(key, 23))
    groups = TOKENS // SEQ_DEV
    per_group = SEQ_DEV // BLOCK
    level = jax.random.randint(first, (groups, groups), 1, 8)
    level = jnp.repeat(jnp.repeat(level, per_group, axis=0), per_group, axis=1)
    rolled = jax.random.randint(second, (NB, NB), 0, 8)
    result = (rolled < level).astype(jnp.int32)
    result = result.at[0, 1].set(0).at[1, 0].set(1)
    return result


def setup_inputs(seed: int = 0) -> dict:
    streams_of = jax.random.split(jax.random.key(seed), 3)
    tokens_qkv = draw_tokens_qkv(jax.random.fold_in(streams_of[2], 71), 0)
    block_mask = draw_block_mask(jax.random.fold_in(streams_of[2], 71), 0)
    return dict(tokens_qkv=tokens_qkv, block_mask=block_mask)


def reference(tokens_qkv, block_mask):
    packed = tokens_qkv.reshape(TOKENS, HEADS, 3, HD)
    by_heads = jnp.transpose(packed, (1, 2, 0, 3))
    blocks = TOKENS // BLOCK
    allowed = (block_mask == 1) | jnp.eye(blocks, dtype=bool)
    allowed = jnp.broadcast_to(allowed[:, None, :, None], (blocks, BLOCK, blocks, BLOCK)).reshape(TOKENS, TOKENS)
    factor_scale = HD ** -0.5

    def one_head(triple):
        scores = jnp.dot(triple[0], triple[1].T, preferred_element_type=jnp.float32) * factor_scale
        scores = jnp.where(allowed, scores, -1e30)
        largest = jnp.max(scores, axis=1, keepdims=True)
        weights = jnp.where(allowed, jnp.exp(scores - largest), 0.0)
        totals = jnp.sum(weights, axis=1, keepdims=True)
        summed = jnp.dot(weights.astype(jnp.bfloat16), triple[2], preferred_element_type=jnp.float32)
        return (summed / totals).astype(jnp.bfloat16)

    outputs = lax.map(one_head, by_heads)
    return jnp.transpose(outputs, (1, 0, 2)).reshape(TOKENS, HEADS * HD)
```

```python
import functools
import math

import jax
import jax.numpy as jnp
from jax import lax
from jax.experimental import pallas as pl
from jax.experimental.pallas import tpu as pltpu
from jax.sharding import PartitionSpec as P

MESH = pl.DeviceIdType.MESH
HD = 128
BLOCK = 128
ROWS = 32
NX, NY, NZ, NC = 4, 4, 8, 2
QUERIES = NY * NZ * ROWS
CHUNK = NX * NC * NY * ROWS
TILE = 256
NEGATIVE = -1e30
EXPONENT = math.log2(math.e) / math.sqrt(HD)


def device_at(x, y, z, c):
    return ((z // 2) * NC + c, y * 8 + (z % 2) * NX + x)


def z_offset(i):
    return ((i + 1) // 2) * (2 * (i % 2) - 1)


def block_of(y, z, c):
    return ((z // 2) * NC + c) * 8 + y * 2 + z % 2


def kernel(
    tokens, mask, out, kv, qa, acc, top, bias, result,
    q_sem, kv_sem, own_send, ring_sem, ring_send, out_sem, out_send,
):
    blk, place = lax.axis_index("blk"), lax.axis_index("head")
    c, y, x = blk % NC, place // 8, place % NX
    z = (blk // NC) * 2 + (place // NX) % 2
    head = y * NZ + z
    right, left, across = (x + 1) % NX, (x + NX - 1) % NX, (x + 2) % NX
    other = 1 - c

    barrier = pltpu.get_barrier_semaphore()

    def peer(t):
        return (y + t % NY) % NY, (z + z_offset(t // NY) + NZ) % NZ

    @pl.loop(1, NY * NZ)
    def _(t):
        py, pz = peer(t)
        pl.semaphore_signal(barrier, inc=1, device_id=device_at(x, py, pz, c), device_id_type=MESH)

    for where in (device_at(left, y, z, c), device_at(right, y, z, c), device_at(x, y, z, other)):
        pl.semaphore_signal(barrier, inc=1, device_id=where, device_id_type=MESH)
    pl.semaphore_wait(barrier, NY * NZ + 2)

    my_rows = pl.ds(pl.multiple_of(y * ROWS, ROWS), ROWS)

    def send_kv(t):
        py, pz = peer(t)
        columns = pl.ds(pl.multiple_of((py * NZ + pz) * 3 * HD + HD, HD), 2 * HD)
        pltpu.make_async_remote_copy(
            src_ref=tokens.at[:, columns],
            dst_ref=kv.at[z, x, c, my_rows, :],
            send_sem=own_send.at[0],
            recv_sem=kv_sem.at[z],
            device_id=device_at(x, py, pz, c),
            device_id_type=MESH,
        ).start()

    def send_q(t):
        py, pz = peer(t)
        columns = pl.ds(pl.multiple_of((py * NZ + pz) * 3 * HD, HD), HD)
        pltpu.make_async_remote_copy(
            src_ref=tokens.at[:, columns],
            dst_ref=qa.at[pl.ds(pl.multiple_of((z * NY + y) * ROWS, ROWS), ROWS), pl.ds(0, HD)],
            send_sem=own_send.at[1],
            recv_sem=q_sem.at[0],
            device_id=device_at(x, py, pz, c),
            device_id_type=MESH,
        ).start()

    pltpu.make_async_copy(
        tokens.at[:, pl.ds(pl.multiple_of(head * 3 * HD + HD, HD), 2 * HD)], kv.at[z, x, c, my_rows, :], kv_sem.at[z]
    ).start()
    pltpu.make_async_copy(
        tokens.at[:, pl.ds(pl.multiple_of(head * 3 * HD, HD), HD)],
        qa.at[pl.ds(pl.multiple_of((z * NY + y) * ROWS, ROWS), ROWS), pl.ds(0, HD)],
        q_sem.at[0],
    ).start()
    pl.loop(1, NY)(send_kv)
    pl.loop(1, NY * NZ)(send_q)
    pl.loop(NY, NY * NZ)(send_kv)

    row_block = lax.broadcasted_iota(jnp.int32, (64, 64), 0)
    col_block = lax.broadcasted_iota(jnp.int32, (64, 64), 1)
    bias[...] = jnp.zeros_like(bias)
    bias[:, 0:64] = jnp.where((mask[...] == 1) | (row_block == col_block), 0.0, NEGATIVE)

    @pl.loop(0, NY * NZ)
    def _(g):
        line = bias[pl.ds(block_of(g % NY, g // NY, c), 1), :]
        rows = pl.ds(pl.multiple_of(g * ROWS, ROWS), ROWS)
        qa[rows, HD : 2 * HD] = jnp.broadcast_to(line, (ROWS, HD)).astype(jnp.bfloat16)

    acc[...] = jnp.zeros_like(acc)
    top[...] = jnp.full_like(top, NEGATIVE)

    def chunk_of(s):
        return (z + NZ - z_offset(s)) % NZ

    def ring(zc, xc, where, send):
        return pltpu.make_async_remote_copy(
            src_ref=kv.at[zc, xc, c],
            dst_ref=kv.at[zc, xc, c],
            send_sem=ring_send.at[send],
            recv_sem=ring_sem.at[zc, xc, c],
            device_id=where,
            device_id_type=MESH,
        )

    def arrived(zc, xc, cc):
        pltpu.make_async_copy(kv.at[zc, xc, cc], kv.at[zc, xc, cc], ring_sem.at[zc, xc, cc]).wait()

    at_right, at_left, at_other = device_at(right, y, z, c), device_at(left, y, z, c), device_at(x, y, z, other)

    def send_tile(j):
        @pl.loop(0, TILE // ROWS)
        def _(g):
            group = j * (TILE // ROWS) + g
            py, pz = group % NY, group // NY
            source = result.at[pl.ds(pl.multiple_of(group * ROWS, ROWS), ROWS), :]
            target = out.at[:, pl.ds(pl.multiple_of(head * HD, HD), HD)]
            mine = (py == y) & (pz == z)

            @pl.when(mine)
            def _():
                pltpu.make_async_copy(source, target, out_sem.at[0]).start()

            @pl.when(jnp.logical_not(mine))
            def _():
                pltpu.make_async_remote_copy(
                    src_ref=source, dst_ref=target, send_sem=out_send.at[0], recv_sem=out_sem.at[0],
                    device_id=device_at(x, py, pz, c), device_id_type=MESH,
                ).start()

    def attend(zc, last):
        row = lax.broadcasted_iota(jnp.int32, (NC * NY * ROWS, HD), 0)
        col = lax.broadcasted_iota(jnp.int32, (NC * NY * ROWS, HD), 1)
        first = (zc // 2) * NC * 8 + zc % 2
        hot = (col == first + (row // (NY * ROWS)) * 8 + ((row // ROWS) % NY) * 2)
        hot = jnp.where(hot, 1.0, 0.0).astype(jnp.bfloat16)
        hot = jnp.concatenate([hot] * NX, axis=0)
        keys = jnp.concatenate([kv[zc, :, :, :, 0:HD].reshape(CHUNK, HD), hot], axis=1)
        values = jnp.concatenate(
            [kv[zc, :, :, :, HD : 2 * HD].reshape(CHUNK, HD), jnp.ones((CHUNK, HD), jnp.bfloat16)], axis=1
        )

        for j in range(QUERIES // TILE):
            rows = slice(j * TILE, (j + 1) * TILE)
            scores = lax.dot_general(
                qa[rows, :], keys, (((1,), (1,)), ((), ())), preferred_element_type=jnp.float32
            )
            old = top[rows, :]
            new = jnp.maximum(old, jnp.max(scores, axis=1, keepdims=True))
            top[rows, :] = new
            weights = jnp.exp2((scores - new[:, 0:1]) * EXPONENT).astype(jnp.bfloat16)
            factor = jnp.exp2((old - new) * EXPONENT)
            acc[rows, :] = acc[rows, :] * jnp.concatenate([factor, factor], axis=1) + jnp.dot(
                weights, values, preferred_element_type=jnp.float32
            )

    @pl.loop(0, NZ + 3)
    def _(s):
        @pl.when(s < NZ)
        def _():
            zc = chunk_of(s)
            pltpu.make_async_copy(kv.at[zc, x, c], kv.at[zc, x, c], kv_sem.at[zc]).wait()
            ring(zc, x, at_right, 0).start()
            ring(zc, x, at_left, 1).start()
            ring(zc, x, at_other, 2).start()

        @pl.when((s >= 1) & (s <= NZ))
        def _():
            zc = chunk_of(s - 1)
            arrived(zc, left, c)
            arrived(zc, right, c)

            @pl.when(s % 2 == 0)
            def _():
                ring(zc, left, at_right, 3).start()

            @pl.when(s % 2 == 1)
            def _():
                ring(zc, right, at_left, 3).start()

            ring(zc, left, at_other, 4).start()
            ring(zc, right, at_other, 5).start()

        @pl.when((s >= 2) & (s <= NZ + 1))
        def _():
            zc = chunk_of(s - 2)
            arrived(zc, across, c)
            ring(zc, across, at_other, 6).start()

        @pl.when(s == 3)
        def _():
            pltpu.make_async_copy(qa.at[:, pl.ds(0, HD)], qa.at[:, pl.ds(0, HD)], q_sem.at[0]).wait()

        @pl.when(s >= 3)
        def _():
            zc = chunk_of(s - 3)
            for xc in range(NX):
                arrived(zc, xc, other)
            attend(zc, s == NZ + 2)

    for j in range(QUERIES // TILE):
        rows = slice(j * TILE, (j + 1) * TILE)
        result[rows, :] = (acc[rows, 0:HD] / acc[rows, HD : 2 * HD]).astype(jnp.bfloat16)
        send_tile(j)

    @pl.loop(0, 7)
    def _(i):
        pltpu.make_async_copy(kv.at[:, 0, 0], kv.at[:, 0, 0], ring_send.at[i]).wait()

    sent = pl.ds(0, QUERIES - ROWS)
    pltpu.make_async_copy(qa.at[sent, :], qa.at[sent, :], own_send.at[0]).wait()
    pltpu.make_async_copy(result.at[sent, :], result.at[sent, :], own_send.at[1]).wait()
    pltpu.make_async_copy(result.at[sent, :], result.at[sent, :], out_send.at[0]).wait()
    pltpu.make_async_copy(result, result, out_sem.at[0]).wait()


def on_device(tokens_qkv, block_mask):
    dma = pltpu.SemaphoreType.DMA
    return pl.pallas_call(
        kernel,
        out_shape=jax.ShapeDtypeStruct((ROWS, NY * NZ * HD), jnp.bfloat16),
        in_specs=[pl.BlockSpec(memory_space=pl.ANY), pl.BlockSpec(memory_space=pltpu.VMEM)],
        out_specs=pl.BlockSpec(memory_space=pl.ANY),
        scratch_shapes=[
            pltpu.VMEM((NZ, NX, NC, NY * ROWS, 2 * HD), jnp.bfloat16),
            pltpu.VMEM((QUERIES, 2 * HD), jnp.bfloat16),
            pltpu.VMEM((QUERIES, 2 * HD), jnp.float32),
            pltpu.VMEM((QUERIES, HD), jnp.float32),
            pltpu.VMEM((64, HD), jnp.float32),
            pltpu.VMEM((QUERIES, HD), jnp.bfloat16),
            dma((1,)),
            dma((NZ,)),
            dma((2,)),
            dma((NZ, NX, NC)),
            dma((7,)),
            dma((1,)),
            dma((1,)),
        ],
        compiler_params=pltpu.CompilerParams(
            collective_id=0, has_side_effects=True, vmem_limit_bytes=48 * 1024 * 1024
        ),
        cost_estimate=pl.CostEstimate(flops=8 * 1024 * 8192 * 128, bytes_accessed=1 << 20, transcendentals=1024 * 8192),
    )(tokens_qkv, block_mask)


def solution(mesh):
    return jax.shard_map(
        on_device,
        mesh=mesh,
        in_specs=(P(("blk", "head"), None), P()),
        out_specs=P(("blk", "head"), None),
        check_vma=False,
    )
```

```python
import functools
import math

import jax
import jax.numpy as jnp
from jax import lax
from jax.experimental import pallas as pl
from jax.experimental.pallas import tpu as pltpu
from jax.sharding import PartitionSpec as P

MESH = pl.DeviceIdType.MESH
HD = 128
BLOCK = 128
ROWS = 32
NX, NY, NZ, NC = 4, 4, 8, 2
QUERIES = NY * NZ * ROWS
LINE = NZ * ROWS
PIECE = NX * NC * LINE
TILE = 256
NEGATIVE = -1e30
EXPONENT = math.log2(math.e) / math.sqrt(HD)


def device_at(x, y, z, c):
    return ((z // 2) * NC + c, y * 8 + (z % 2) * NX + x)


def block_of(y, z, c):
    return ((z // 2) * NC + c) * 8 + y * 2 + z % 2


def aligned(start, size):
    return pl.ds(pl.multiple_of(start, size), size)


def kernel(
    tokens, mask, out, held, pairs, stage, kv, qa, acc, top, bias, result,
    in_sem, y_sem, y_send, q_sem, kv_sem, z_send, ring_sem, ring_send, out_sem, out_send,
):
    blk, place = lax.axis_index("blk"), lax.axis_index("head")
    c, y, x = blk % NC, place // 8, place % NX
    z = (blk // NC) * 2 + (place // NX) % 2
    head = y * NZ + z
    right, left, across = (x + 1) % NX, (x + NX - 1) % NX, (x + 2) % NX
    other = 1 - c
    source = (y, (y + 1) % NY, (y + NY - 1) % NY, (y + 2) % NY)
    at_y = (None, device_at(x, source[2], z, c), device_at(x, source[1], z, c), device_at(x, source[3], z, c))
    z_there = [(z + step) % NZ for step in (1, 7, 2, 6, 3, 5, 4)]
    at_z = [device_at(x, y, there, c) for there in z_there]
    at_right, at_left, at_other = device_at(right, y, z, c), device_at(left, y, z, c), device_at(x, y, z, other)

    load = pltpu.make_async_copy(tokens, held, in_sem.at[0])
    load.start()
    load_mask = pltpu.make_async_copy(mask, pairs, in_sem.at[1])
    load_mask.start()

    barrier = pltpu.get_barrier_semaphore()
    for where in [at_other, at_right, at_left] + list(at_y[1:]) + at_z:
        pl.semaphore_signal(barrier, inc=1, device_id=where, device_id_type=MESH)

    load_mask.wait()
    row_block = lax.broadcasted_iota(jnp.int32, (64, 64), 0)
    col_block = lax.broadcasted_iota(jnp.int32, (64, 64), 1)
    bias[...] = jnp.zeros_like(bias)
    bias[:, 0:64] = jnp.where((pairs[...] == 1) | (row_block == col_block), 0.0, NEGATIVE)

    @pl.loop(0, NY * NZ)
    def _(g):
        line = bias[pl.ds(block_of(g // NZ, g % NZ, c), 1), :]
        qa[aligned(g * ROWS, ROWS), HD : 2 * HD] = jnp.broadcast_to(line, (ROWS, HD)).astype(jnp.bfloat16)

    acc[...] = jnp.zeros_like(acc)
    top[...] = jnp.full_like(top, NEGATIVE)
    load.wait()
    pl.semaphore_wait(barrier, NY + NZ + 1)

    wide = NZ * 3 * HD

    def along_y(k):
        pltpu.make_async_remote_copy(
            src_ref=held.at[:, aligned(source[(0, 2, 1, 3)[k]] * wide, wide)],
            dst_ref=stage.at[k - 1],
            send_sem=y_send.at[0],
            recv_sem=y_sem.at[k - 1],
            device_id=at_y[k],
            device_id_type=MESH,
        ).start()

    def from_y(k):
        pltpu.make_async_copy(stage.at[k - 1], stage.at[k - 1], y_sem.at[k - 1]).wait()

    my_rows = aligned(z * ROWS, ROWS)

    def slab(k, there, part):
        width = 2 * HD if part == 0 else HD
        start = there * 3 * HD + (HD if part == 0 else 0)
        if k == 0:
            return held.at[:, pl.ds(pl.multiple_of(y * wide + start, HD), width)]
        return stage.at[k - 1, :, pl.ds(pl.multiple_of(start, HD), width)]

    def landing(k, part):
        if part == 0:
            return kv.at[source[k], x, c, my_rows, :]
        return qa.at[aligned((source[k] * NZ + z) * ROWS, ROWS), pl.ds(0, HD)]

    def along_z(k, part):
        sem = kv_sem.at[k] if part == 0 else q_sem.at[0]
        for i in range(NZ - 1):
            pltpu.make_async_remote_copy(
                src_ref=slab(k, z_there[i], part),
                dst_ref=landing(k, part),
                send_sem=z_send.at[part],
                recv_sem=sem,
                device_id=at_z[i],
                device_id_type=MESH,
            ).start()
        pltpu.make_async_copy(slab(k, z, part), landing(k, part), sem).start()

    def ring(ref, sem, where, send):
        pltpu.make_async_remote_copy(
            src_ref=ref, dst_ref=ref, send_sem=ring_send.at[send], recv_sem=sem, device_id=where, device_id_type=MESH
        ).start()

    def pick(p):
        return lax.rem(y + (p + 1) // 2 * (2 * (p % 2) - 1) + NY, NY)

    def arrived(yp, xc, cc):
        ref = kv.at[yp, xc, cc]
        pltpu.make_async_copy(ref, ref, ring_sem.at[yp, xc, cc]).wait()

    def step_a(p):
        yp = source[p]
        ref = kv.at[yp, x, c]
        pltpu.make_async_copy(ref, ref, kv_sem.at[p]).wait()
        ring(ref, ring_sem.at[yp, x, c], at_right, 0)
        ring(ref, ring_sem.at[yp, x, c], at_left, 1)
        ring(ref, ring_sem.at[yp, x, c], at_other, 2)

    def step_b(p):
        yp = source[p]
        for xc, half, onward, send in ((left, 0, at_right, 3), (right, 1, at_left, 4)):
            arrived(yp, xc, c)
            ring(kv.at[yp, xc, c, pl.ds(half * (LINE // 2), LINE // 2), :], ring_sem.at[yp, xc, c], onward, send)
        ring(kv.at[yp, left, c], ring_sem.at[yp, left, c], at_other, 5)
        ring(kv.at[yp, right, c], ring_sem.at[yp, right, c], at_other, 6)

    def step_c(p):
        yp = source[p]
        arrived(yp, across, c)
        ring(kv.at[yp, across, c], ring_sem.at[yp, across, c], at_other, 7)

    def send_tile(j):
        target = out.at[:, aligned(head * HD, HD)]

        @pl.loop(0, NZ)
        def _(pz):
            piece = result.at[aligned((j * NZ + pz) * ROWS, ROWS), :]
            mine = (j == y) & (pz == z)

            @pl.when(mine)
            def _():
                pltpu.make_async_copy(piece, target, out_sem.at[0]).start()

            @pl.when(jnp.logical_not(mine))
            def _():
                pltpu.make_async_remote_copy(
                    src_ref=piece, dst_ref=target, send_sem=out_send.at[0], recv_sem=out_sem.at[0],
                    device_id=device_at(x, j, pz, c), device_id_type=MESH,
                ).start()

    def attend(yp, start, tiles, finish):
        row = lax.broadcasted_iota(jnp.int32, (NC * LINE, HD), 0)
        col = lax.broadcasted_iota(jnp.int32, (NC * LINE, HD), 1)
        z_row = (row // ROWS) % NZ
        hot = col == block_of(yp, z_row, row // LINE)
        hot = jnp.where(hot, 1.0, 0.0).astype(jnp.bfloat16)
        hot = jnp.concatenate([hot] * NX, axis=0)
        keys = jnp.concatenate([kv[yp, :, :, :, 0:HD].reshape(PIECE, HD), hot], axis=1)
        values = jnp.concatenate(
            [kv[yp, :, :, :, HD : 2 * HD].reshape(PIECE, HD), jnp.ones((PIECE, HD), jnp.bfloat16)], axis=1
        )

        def place_of(j):
            return aligned(start + j * TILE, TILE)

        def score(j):
            return lax.dot_general(
                qa[place_of(j), :], keys, (((1,), (1,)), ((), ())), preferred_element_type=jnp.float32
            )

        ahead = score(0)
        for j in range(tiles):
            rows = place_of(j)
            scores = ahead
            if j + 1 < tiles:
                ahead = score(j + 1)
            old = top[rows, :]
            new = jnp.maximum(old, jnp.max(scores, axis=1, keepdims=True))
            top[rows, :] = new
            weights = jnp.exp2((scores - new[:, 0:1]) * EXPONENT).astype(jnp.bfloat16)
            factor = jnp.exp2((old - new) * EXPONENT)
            total = acc[rows, :] * jnp.concatenate([factor, factor], axis=1) + jnp.dot(
                weights, values, preferred_element_type=jnp.float32
            )
            if finish:
                result[rows, :] = (total[:, 0:HD] / total[:, HD : 2 * HD]).astype(jnp.bfloat16)
                send_tile(j)
            else:
                acc[rows, :] = total

    along_y(1)
    along_y(2)
    along_z(0, 1)
    along_z(0, 0)
    from_y(1)
    along_z(1, 1)
    along_z(1, 0)
    from_y(2)
    along_y(3)
    along_z(2, 1)
    step_a(0)
    from_y(3)
    along_z(3, 1)
    along_z(2, 0)
    along_z(3, 0)
    step_b(0)
    step_a(1)
    step_c(0)
    step_b(1)
    queries = qa.at[:, pl.ds(0, HD)]
    pltpu.make_async_copy(queries, queries, q_sem.at[0]).wait()

    @pl.loop(0, 6)
    def _(i):
        p = i // 2

        @pl.when(i == 2)
        def _():
            step_a(2)
            step_c(1)

        @pl.when(i == 4)
        def _():
            step_a(3)
            step_b(2)
            step_c(2)

        @pl.when(i == 5)
        def _():
            step_b(3)

        @pl.when(i % 2 == 0)
        def _():
            for xc in range(NX):
                arrived(pick(p), xc, other)

        attend(pick(p), (i % 2) * (QUERIES // 2), QUERIES // 2 // TILE, False)

    step_c(3)
    for xc in range(NX):
        arrived(source[3], xc, other)
    attend(source[3], 0, QUERIES // TILE, True)

    def done(ref, sem):
        pltpu.make_async_copy(ref, ref, sem).wait()

    done(stage, y_send.at[0])
    done(qa.at[pl.ds(0, QUERIES - NY * ROWS), :], z_send.at[0])
    done(result.at[pl.ds(0, QUERIES - NY * ROWS), :], z_send.at[1])
    for i in range(8):
        ref = kv.at[:, 0, 0, pl.ds(0, LINE // 2), :] if i in (3, 4) else kv.at[:, 0, 0]
        done(ref, ring_send.at[i])
    done(result.at[pl.ds(0, QUERIES - ROWS), :], out_send.at[0])
    done(result, out_sem.at[0])


def on_device(tokens_qkv, block_mask):
    dma = pltpu.SemaphoreType.DMA
    return pl.pallas_call(
        kernel,
        out_shape=jax.ShapeDtypeStruct((ROWS, NY * NZ * HD), jnp.bfloat16),
        in_specs=[pl.BlockSpec(memory_space=pl.ANY), pl.BlockSpec(memory_space=pl.ANY)],
        out_specs=pl.BlockSpec(memory_space=pl.ANY),
        scratch_shapes=[
            pltpu.VMEM((ROWS, NY * NZ * 3 * HD), jnp.bfloat16),
            pltpu.VMEM((64, 64), jnp.int32),
            pltpu.VMEM((NY - 1, ROWS, NZ * 3 * HD), jnp.bfloat16),
            pltpu.VMEM((NY, NX, NC, LINE, 2 * HD), jnp.bfloat16),
            pltpu.VMEM((QUERIES, 2 * HD), jnp.bfloat16),
            pltpu.VMEM((QUERIES, 2 * HD), jnp.float32),
            pltpu.VMEM((QUERIES, HD), jnp.float32),
            pltpu.VMEM((64, HD), jnp.float32),
            pltpu.VMEM((QUERIES, HD), jnp.bfloat16),
            dma((2,)),
            dma((NY - 1,)),
            dma((1,)),
            dma((1,)),
            dma((NY,)),
            dma((2,)),
            dma((NY, NX, NC)),
            dma((8,)),
            dma((1,)),
            dma((1,)),
        ],
        compiler_params=pltpu.CompilerParams(
            collective_id=0, has_side_effects=True, vmem_limit_bytes=62 * 1024 * 1024
        ),
        cost_estimate=pl.CostEstimate(flops=8 * 1024 * 8192 * 128, bytes_accessed=1 << 20, transcendentals=1024 * 8192),
    )(tokens_qkv, block_mask)


def solution(mesh):
    return jax.shard_map(
        on_device,
        mesh=mesh,
        in_specs=(P(("blk", "head"), None), P()),
        out_specs=P(("blk", "head"), None),
        check_vma=False,
    )
```

```python
import functools
import math

import jax
import jax.numpy as jnp
from jax import lax
from jax.experimental import pallas as pl
from jax.experimental.pallas import tpu as pltpu
from jax.sharding import PartitionSpec as P

MESH = pl.DeviceIdType.MESH
HD = 128
BLOCK = 128
ROWS = 32
NX, NY, NZ, NC = 4, 4, 8, 2
QUERIES = NY * NZ * ROWS
HALF = ROWS // 2
LINE = NZ * HALF
PIECE = 2 * NX * NC * LINE
TILE = 256
NEGATIVE = -1e30
EXPONENT = math.log2(math.e) / math.sqrt(HD)


BEFORE = (
    "Y1Y2K0Q0y1y2A0W1K1w1Q1W2K2Y3y3w2",
    "Q2W3K3w3Q3A1A2A3B0B1A4A5B2B3C0C1",
)
STEPS = ("A6S0R0R1", "A7B4B5C2C3S1", "B6R2R3", "B7C4C5", "C6S2", "C7")
AFTER = "S3"


def device_at(x, y, z, c):
    return ((z // 2) * NC + c, y * 8 + (z % 2) * NX + x)


def block_of(y, z, c):
    return ((z // 2) * NC + c) * 8 + y * 2 + z % 2


def aligned(start, size):
    return pl.ds(pl.multiple_of(start, size), size)


def kernel(
    tokens, mask, out, held, pairs, stage, kv, qa, acc, top, bias, result,
    in_sem, y_sem, y_send, q_sem, kv_sem, z_send, ring_sem, ring_send, out_sem, out_send,
):
    blk, place = lax.axis_index("blk"), lax.axis_index("head")
    c, y, x = blk % NC, place // 8, place % NX
    z = (blk // NC) * 2 + (place // NX) % 2
    head = y * NZ + z
    right, left, across = (x + 1) % NX, (x + NX - 1) % NX, (x + 2) % NX
    other = 1 - c
    source = (y, (y + 1) % NY, (y + NY - 1) % NY, (y + 2) % NY)
    at_y = (None, device_at(x, source[2], z, c), device_at(x, source[1], z, c), device_at(x, source[3], z, c))
    z_there = [(z + step) % NZ for step in (1, 7, 2, 6, 3, 5, 4)]
    at_z = [device_at(x, y, there, c) for there in z_there]
    at_right, at_left, at_other = device_at(right, y, z, c), device_at(left, y, z, c), device_at(x, y, z, other)

    load = pltpu.make_async_copy(tokens, held, in_sem.at[0])
    load.start()
    load_mask = pltpu.make_async_copy(mask, pairs, in_sem.at[1])
    load_mask.start()

    barrier = pltpu.get_barrier_semaphore()
    for where in [at_other, at_right, at_left] + list(at_y[1:]) + at_z:
        pl.semaphore_signal(barrier, inc=1, device_id=where, device_id_type=MESH)

    load_mask.wait()
    row_block = lax.broadcasted_iota(jnp.int32, (64, 64), 0)
    col_block = lax.broadcasted_iota(jnp.int32, (64, 64), 1)
    bias[...] = jnp.zeros_like(bias)
    bias[:, 0:64] = jnp.where((pairs[...] == 1) | (row_block == col_block), 0.0, NEGATIVE)

    @pl.loop(0, NY * NZ)
    def _(g):
        line = bias[pl.ds(block_of(g // NZ, g % NZ, c), 1), :]
        qa[aligned(g * ROWS, ROWS), HD : 2 * HD] = jnp.broadcast_to(line, (ROWS, HD)).astype(jnp.bfloat16)

    acc[...] = jnp.zeros_like(acc)
    top[...] = jnp.full_like(top, NEGATIVE)
    load.wait()
    pl.semaphore_wait(barrier, NY + NZ + 1)

    wide = NZ * 3 * HD

    def along_y(k, part):
        there = source[(0, 2, 1, 3)[k]]
        for i in range(NZ):
            start = (z_there[i] if i < NZ - 1 else z) * 3 * HD + (HD if part == 0 else 0)
            width = 2 * HD if part == 0 else HD
            pltpu.make_async_remote_copy(
                src_ref=held.at[:, pl.ds(pl.multiple_of(there * wide + start, HD), width)],
                dst_ref=stage.at[k - 1, :, pl.ds(pl.multiple_of(start, HD), width)],
                send_sem=y_send.at[part],
                recv_sem=y_sem.at[k - 1, part],
                device_id=at_y[k],
                device_id_type=MESH,
            ).start()

    def from_y(k, part):
        ref = stage.at[k - 1, :, pl.ds(0, NZ * (HD if part else 2 * HD))]
        pltpu.make_async_copy(ref, ref, y_sem.at[k - 1, part]).wait()

    def slab(k, there, part):
        width = HD if part == 2 else 2 * HD
        start = there * 3 * HD + (0 if part == 2 else HD)
        rows = pl.ds(0, ROWS) if part == 2 else pl.ds(part * HALF, HALF)
        if k == 0:
            return held.at[rows, pl.ds(pl.multiple_of(y * wide + start, HD), width)]
        return stage.at[k - 1, rows, pl.ds(pl.multiple_of(start, HD), width)]

    def landing(k, part):
        if part < 2:
            return kv.at[source[k], part, x, c, aligned(z * HALF, HALF), :]
        return qa.at[aligned((source[k] * NZ + z) * ROWS, ROWS), pl.ds(0, HD)]

    def along_z(k, part):
        sem = kv_sem.at[k, part] if part < 2 else q_sem.at[k]
        for i in range(NZ - 1):
            pltpu.make_async_remote_copy(
                src_ref=slab(k, z_there[i], part),
                dst_ref=landing(k, part),
                send_sem=z_send.at[part // 2],
                recv_sem=sem,
                device_id=at_z[i],
                device_id_type=MESH,
            ).start()
        pltpu.make_async_copy(slab(k, z, part), landing(k, part), sem).start()

    def ring(ref, sem, where, send):
        pltpu.make_async_remote_copy(
            src_ref=ref, dst_ref=ref, send_sem=ring_send.at[send], recv_sem=sem, device_id=where, device_id_type=MESH
        ).start()

    def pick(p):
        return lax.rem(y + (p + 1) // 2 * (2 * (p % 2) - 1) + NY, NY)

    def arrived(yp, h, xc, cc):
        ref = kv.at[yp, h, xc, cc]
        pltpu.make_async_copy(ref, ref, ring_sem.at[yp, h, xc, cc]).wait()

    def step_a(p):
        yp, h = source[p // 2], p % 2
        ref, sem = kv.at[yp, h, x, c], ring_sem.at[yp, h, x, c]
        pltpu.make_async_copy(ref, ref, kv_sem.at[p // 2, h]).wait()
        ring(ref, sem, at_right, 0)
        ring(ref, sem, at_left, 1)
        ring(ref, sem, at_other, 2)

    def step_b(p):
        yp, h = source[p // 2], p % 2
        for xc, half, onward, send in ((left, 0, at_right, 3), (right, 1, at_left, 4)):
            arrived(yp, h, xc, c)
            ring(kv.at[yp, h, xc, c, pl.ds(half * (LINE // 2), LINE // 2), :], ring_sem.at[yp, h, xc, c], onward, send)
        ring(kv.at[yp, h, left, c], ring_sem.at[yp, h, left, c], at_other, 5)
        ring(kv.at[yp, h, right, c], ring_sem.at[yp, h, right, c], at_other, 6)

    def step_c(p):
        yp, h = source[p // 2], p % 2
        arrived(yp, h, across, c)
        ring(kv.at[yp, h, across, c], ring_sem.at[yp, h, across, c], at_other, 7)

    def complete(k):
        for h in range(2):
            for xc in range(NX):
                arrived(source[k], h, xc, other)

    def send_tile(j):
        target = out.at[:, aligned(head * HD, HD)]

        @pl.loop(0, NZ)
        def _(pz):
            piece = result.at[aligned((j * NZ + pz) * ROWS, ROWS), :]
            mine = (j == y) & (pz == z)

            @pl.when(mine)
            def _():
                pltpu.make_async_copy(piece, target, out_sem.at[0]).start()

            @pl.when(jnp.logical_not(mine))
            def _():
                pltpu.make_async_remote_copy(
                    src_ref=piece, dst_ref=target, send_sem=out_send.at[0], recv_sem=out_sem.at[0],
                    device_id=device_at(x, j, pz, c), device_id_type=MESH,
                ).start()

    def attend(k, half, finish):
        yp = pick(k)
        row = lax.broadcasted_iota(jnp.int32, (NC * LINE, HD), 0)
        col = lax.broadcasted_iota(jnp.int32, (NC * LINE, HD), 1)
        hot = col == block_of(yp, (row // HALF) % NZ, row // LINE)
        hot = jnp.where(hot, 1.0, 0.0).astype(jnp.bfloat16)
        hot = jnp.concatenate([hot] * (2 * NX), axis=0)
        keys = jnp.concatenate([kv[yp, :, :, :, :, 0:HD].reshape(PIECE, HD), hot], axis=1)
        values = jnp.concatenate(
            [kv[yp, :, :, :, :, HD : 2 * HD].reshape(PIECE, HD), jnp.ones((PIECE, HD), jnp.bfloat16)], axis=1
        )

        def score(place):
            return lax.dot_general(
                qa[aligned(place * TILE, TILE), :], keys, (((1,), (1,)), ((), ())), preferred_element_type=jnp.float32
            )

        places = [pick(half * 2), pick(half * 2 + 1)]
        ahead = score(places[0])
        for j, place in enumerate(places):
            rows = aligned(place * TILE, TILE)
            scores = ahead
            if j + 1 < len(places):
                ahead = score(places[j + 1])
            old = top[rows, :]
            new = jnp.maximum(old, jnp.max(scores, axis=1, keepdims=True))
            top[rows, :] = new
            weights = jnp.exp2((scores - new[:, 0:1]) * EXPONENT).astype(jnp.bfloat16)
            factor = jnp.exp2((old - new) * EXPONENT)
            total = acc[rows, :] * jnp.concatenate([factor, factor], axis=1) + jnp.dot(
                weights, values, preferred_element_type=jnp.float32
            )
            if finish:
                result[rows, :] = (total[:, 0:HD] / total[:, HD : 2 * HD]).astype(jnp.bfloat16)
                send_tile(place)
            else:
                acc[rows, :] = total

    def queries(k):
        ref = qa.at[aligned(source[k] * TILE, TILE), pl.ds(0, HD)]
        pltpu.make_async_copy(ref, ref, q_sem.at[k]).wait()

    def keys_of(k):
        along_z(k, 0)
        along_z(k, 1)

    actions = dict(

        A=step_a, B=step_b, C=step_c, K=keys_of, Q=lambda k: along_z(k, 2), S=complete, R=queries,
        Y=lambda k: along_y(k, 0), y=lambda k: along_y(k, 1), W=lambda k: from_y(k, 0), w=lambda k: from_y(k, 1),
    )

    def run(text):
        for action, which in zip(text[::2], text[1::2]):
            actions[action](int(which))

    for text in BEFORE:
        run(text)

    @pl.loop(0, 6)
    def _(i):
        for at, text in enumerate(STEPS):

            @pl.when(i == at)
            def _():
                run(text)

        attend(jnp.where(i < 4, i % 2, 2), jnp.where(i < 4, i // 2, i % 2), False)

    run(AFTER)

    @pl.loop(0, 2)
    def _(half):
        attend(3, half, True)

    def done(ref, sem):
        pltpu.make_async_copy(ref, ref, sem).wait()

    done(stage.at[:, :, pl.ds(0, NZ * 2 * HD)], y_send.at[0])
    done(stage.at[:, :, pl.ds(0, NZ * HD)], y_send.at[1])
    done(qa.at[pl.ds(0, QUERIES - NY * ROWS), :], z_send.at[0])
    done(result.at[pl.ds(0, QUERIES - NY * ROWS), :], z_send.at[1])
    for i in range(8):
        ref = kv.at[:, :, 0, 0, pl.ds(0, LINE // 2), :] if i in (3, 4) else kv.at[:, :, 0, 0]
        done(ref, ring_send.at[i])
    done(result.at[pl.ds(0, QUERIES - ROWS), :], out_send.at[0])
    done(result, out_sem.at[0])


def on_device(tokens_qkv, block_mask):
    dma = pltpu.SemaphoreType.DMA
    return pl.pallas_call(
        kernel,
        out_shape=jax.ShapeDtypeStruct((ROWS, NY * NZ * HD), jnp.bfloat16),
        in_specs=[pl.BlockSpec(memory_space=pl.ANY), pl.BlockSpec(memory_space=pl.ANY)],
        out_specs=pl.BlockSpec(memory_space=pl.ANY),
        scratch_shapes=[
            pltpu.VMEM((ROWS, NY * NZ * 3 * HD), jnp.bfloat16),
            pltpu.VMEM((64, 64), jnp.int32),
            pltpu.VMEM((NY - 1, ROWS, NZ * 3 * HD), jnp.bfloat16),
            pltpu.VMEM((NY, 2, NX, NC, LINE, 2 * HD), jnp.bfloat16),
            pltpu.VMEM((QUERIES, 2 * HD), jnp.bfloat16),
            pltpu.VMEM((QUERIES, 2 * HD), jnp.float32),
            pltpu.VMEM((QUERIES, HD), jnp.float32),
            pltpu.VMEM((64, HD), jnp.float32),
            pltpu.VMEM((QUERIES, HD), jnp.bfloat16),
            dma((2,)),
            dma((NY - 1, 2)),
            dma((2,)),
            dma((NY,)),
            dma((NY, 2)),
            dma((2,)),
            dma((NY, 2, NX, NC)),
            dma((8,)),
            dma((1,)),
            dma((1,)),
        ],
        compiler_params=pltpu.CompilerParams(
            collective_id=0, has_side_effects=True, vmem_limit_bytes=62 * 1024 * 1024
        ),
        cost_estimate=pl.CostEstimate(flops=8 * 1024 * 8192 * 128, bytes_accessed=1 << 20, transcendentals=1024 * 8192),
    )(tokens_qkv, block_mask)


def solution(mesh):
    return jax.shard_map(
        on_device,
        mesh=mesh,
        in_specs=(P(("blk", "head"), None), P()),
        out_specs=P(("blk", "head"), None),
        check_vma=False,
    )
```

```python
import functools
import math

import jax
import jax.numpy as jnp
from jax import lax
from jax.experimental import pallas as pl
from jax.experimental.pallas import tpu as pltpu
from jax.sharding import PartitionSpec as P

MESH = pl.DeviceIdType.MESH
HD = 128
BLOCK = 128
ROWS = 32
NX, NY, NZ, NC = 4, 4, 8, 2
QUERIES = NY * NZ * ROWS
HALF = ROWS // 2
LINE = NZ * HALF
PIECE = 2 * NX * NC * LINE
TILE = 256
NEGATIVE = -1e30
EXPONENT = math.log2(math.e) / math.sqrt(HD)


BEFORE = (
    "Y1Y2K0Q0y1y2A0W1K1w1Q1W2K2Y3y3w2",
    "Q2W3K3w3Q3A1A2A3B0B1A4A5B2B3C0C1",
)
STEPS = ("A6S0R0R1", "A7B4B5C2C3S1", "B6R2R3", "B7C4C5", "C6S2", "C7")
AFTER = "S3"


def device_at(x, y, z, c):
    return ((z // 2) * NC + c, y * 8 + (z % 2) * NX + x)


def block_of(y, z, c):
    return ((z // 2) * NC + c) * 8 + y * 2 + z % 2


def aligned(start, size):
    return pl.ds(pl.multiple_of(start, size), size)


def kernel(
    tokens, mask, out, held, pairs, stage, kv, qa, acc, top, bias, result,
    in_sem, y_sem, y_send, q_sem, kv_sem, z_send, ring_sem, ring_send, out_sem, out_send,
):
    blk, place = lax.axis_index("blk"), lax.axis_index("head")
    c, y, x = blk % NC, place // 8, place % NX
    z = (blk // NC) * 2 + (place // NX) % 2
    head = y * NZ + z
    right, left, across = (x + 1) % NX, (x + NX - 1) % NX, (x + 2) % NX
    other = 1 - c
    source = (y, (y + 1) % NY, (y + NY - 1) % NY, (y + 2) % NY)
    at_y = (None, device_at(x, source[2], z, c), device_at(x, source[1], z, c), device_at(x, source[3], z, c))
    z_there = [(z + step) % NZ for step in (1, 7, 2, 6, 3, 5, 4)]
    at_z = [device_at(x, y, there, c) for there in z_there]
    at_right, at_left, at_other = device_at(right, y, z, c), device_at(left, y, z, c), device_at(x, y, z, other)

    load = pltpu.make_async_copy(tokens, held, in_sem.at[0])
    load.start()
    load_mask = pltpu.make_async_copy(mask, pairs, in_sem.at[1])
    load_mask.start()

    barrier = pltpu.get_barrier_semaphore()
    for where in [at_other, at_right, at_left] + list(at_y[1:]) + at_z:
        pl.semaphore_signal(barrier, inc=1, device_id=where, device_id_type=MESH)

    load_mask.wait()
    row_block = lax.broadcasted_iota(jnp.int32, (64, 64), 0)
    col_block = lax.broadcasted_iota(jnp.int32, (64, 64), 1)
    bias[...] = jnp.zeros_like(bias)
    bias[:, 0:64] = jnp.where((pairs[...] == 1) | (row_block == col_block), 0.0, NEGATIVE)

    @pl.loop(0, NY * NZ)
    def _(g):
        line = bias[pl.ds(block_of(g // NZ, g % NZ, c), 1), :]
        qa[aligned(g * ROWS, ROWS), HD : 2 * HD] = jnp.broadcast_to(line, (ROWS, HD)).astype(jnp.bfloat16)

    acc[...] = jnp.zeros_like(acc)
    top[...] = jnp.full_like(top, NEGATIVE)
    load.wait()
    pl.semaphore_wait(barrier, NY + NZ + 1)

    wide = NZ * 3 * HD

    def along_y(k, part):
        there = source[(0, 2, 1, 3)[k]]
        for i in range(NZ):
            start = (z_there[i] if i < NZ - 1 else z) * 3 * HD + (HD if part == 0 else 0)
            width = 2 * HD if part == 0 else HD
            pltpu.make_async_remote_copy(
                src_ref=held.at[:, pl.ds(pl.multiple_of(there * wide + start, HD), width)],
                dst_ref=stage.at[k - 1, :, pl.ds(pl.multiple_of(start, HD), width)],
                send_sem=y_send.at[part],
                recv_sem=y_sem.at[k - 1, part],
                device_id=at_y[k],
                device_id_type=MESH,
            ).start()

    def from_y(k, part):
        ref = stage.at[k - 1, :, pl.ds(0, NZ * (HD if part else 2 * HD))]
        pltpu.make_async_copy(ref, ref, y_sem.at[k - 1, part]).wait()

    def slab(k, there, part):
        width = HD if part == 2 else 2 * HD
        start = there * 3 * HD + (0 if part == 2 else HD)
        rows = pl.ds(0, ROWS) if part == 2 else pl.ds(part * HALF, HALF)
        if k == 0:
            return held.at[rows, pl.ds(pl.multiple_of(y * wide + start, HD), width)]
        return stage.at[k - 1, rows, pl.ds(pl.multiple_of(start, HD), width)]

    def landing(k, part):
        if part < 2:
            return kv.at[source[k], part, x, c, aligned(z * HALF, HALF), :]
        return qa.at[aligned((source[k] * NZ + z) * ROWS, ROWS), pl.ds(0, HD)]

    def along_z(k, part):
        sem = kv_sem.at[k, part] if part < 2 else q_sem.at[k]
        for i in range(NZ - 1):
            pltpu.make_async_remote_copy(
                src_ref=slab(k, z_there[i], part),
                dst_ref=landing(k, part),
                send_sem=z_send.at[part // 2],
                recv_sem=sem,
                device_id=at_z[i],
                device_id_type=MESH,
            ).start()
        pltpu.make_async_copy(slab(k, z, part), landing(k, part), sem).start()

    def ring(ref, sem, where, send):
        pltpu.make_async_remote_copy(
            src_ref=ref, dst_ref=ref, send_sem=ring_send.at[send], recv_sem=sem, device_id=where, device_id_type=MESH
        ).start()

    def pick(p):
        return lax.rem(y + (p + 1) // 2 * (2 * (p % 2) - 1) + NY, NY)

    def arrived(yp, h, xc, cc):
        ref = kv.at[yp, h, xc, cc]
        pltpu.make_async_copy(ref, ref, ring_sem.at[yp, h, xc, cc]).wait()

    def step_a(p):
        yp, h = source[p // 2], p % 2
        ref, sem = kv.at[yp, h, x, c], ring_sem.at[yp, h, x, c]
        pltpu.make_async_copy(ref, ref, kv_sem.at[p // 2, h]).wait()
        ring(ref, sem, at_right, 0)
        ring(ref, sem, at_left, 1)
        ring(ref, sem, at_other, 2)

    def step_b(p):
        yp, h = source[p // 2], p % 2
        for xc, half, onward, send in ((left, 0, at_right, 3), (right, 1, at_left, 4)):
            arrived(yp, h, xc, c)
            ring(kv.at[yp, h, xc, c, pl.ds(half * (LINE // 2), LINE // 2), :], ring_sem.at[yp, h, xc, c], onward, send)
        ring(kv.at[yp, h, left, c], ring_sem.at[yp, h, left, c], at_other, 5)
        ring(kv.at[yp, h, right, c], ring_sem.at[yp, h, right, c], at_other, 6)

    def step_c(p):
        yp, h = source[p // 2], p % 2
        arrived(yp, h, across, c)
        ring(kv.at[yp, h, across, c], ring_sem.at[yp, h, across, c], at_other, 7)

    def complete(k):
        for h in range(2):
            for xc in range(NX):
                arrived(source[k], h, xc, other)

    def send_tile(j):
        target = out.at[:, aligned(head * HD, HD)]

        @pl.loop(0, NZ)
        def _(pz):
            piece = result.at[aligned((j * NZ + pz) * ROWS, ROWS), :]
            mine = (j == y) & (pz == z)

            @pl.when(mine)
            def _():
                pltpu.make_async_copy(piece, target, out_sem.at[0]).start()

            @pl.when(jnp.logical_not(mine))
            def _():
                pltpu.make_async_remote_copy(
                    src_ref=piece, dst_ref=target, send_sem=out_send.at[0], recv_sem=out_sem.at[0],
                    device_id=device_at(x, j, pz, c), device_id_type=MESH,
                ).start()

    def attend(k, tiles, finish):
        yp = pick(k)
        row = lax.broadcasted_iota(jnp.int32, (NC * LINE, HD), 0)
        col = lax.broadcasted_iota(jnp.int32, (NC * LINE, HD), 1)
        hot = col == block_of(yp, (row // HALF) % NZ, row // LINE)
        hot = jnp.where(hot, 1.0, 0.0).astype(jnp.bfloat16)
        hot = jnp.concatenate([hot] * (2 * NX), axis=0)
        keys = jnp.concatenate([kv[yp, :, :, :, :, 0:HD].reshape(PIECE, HD), hot], axis=1)
        values = jnp.concatenate(
            [kv[yp, :, :, :, :, HD : 2 * HD].reshape(PIECE, HD), jnp.ones((PIECE, HD), jnp.bfloat16)], axis=1
        )

        def score(place):
            return lax.dot_general(
                qa[aligned(place * TILE, TILE), :], keys, (((1,), (1,)), ((), ())), preferred_element_type=jnp.float32
            )

        places = [pick(t) for t in tiles]
        ahead = score(places[0])
        for j, place in enumerate(places):
            rows = aligned(place * TILE, TILE)
            scores = ahead
            if j + 1 < len(places):
                ahead = score(places[j + 1])
            old = top[rows, :]
            new = jnp.maximum(old, jnp.max(scores, axis=1, keepdims=True))
            top[rows, :] = new
            weights = jnp.exp2((scores - new[:, 0:1]) * EXPONENT).astype(jnp.bfloat16)
            factor = jnp.exp2((old - new) * EXPONENT)
            total = acc[rows, :] * jnp.concatenate([factor, factor], axis=1) + jnp.dot(
                weights, values, preferred_element_type=jnp.float32
            )
            if finish:
                result[rows, :] = (total[:, 0:HD] / total[:, HD : 2 * HD]).astype(jnp.bfloat16)
                send_tile(place)
            else:
                acc[rows, :] = total

    def queries(k):
        ref = qa.at[aligned(source[k] * TILE, TILE), pl.ds(0, HD)]
        pltpu.make_async_copy(ref, ref, q_sem.at[k]).wait()

    def keys_of(k):
        along_z(k, 0)
        along_z(k, 1)

    actions = dict(

        A=step_a, B=step_b, C=step_c, K=keys_of, Q=lambda k: along_z(k, 2), S=complete, R=queries,
        Y=lambda k: along_y(k, 0), y=lambda k: along_y(k, 1), W=lambda k: from_y(k, 0), w=lambda k: from_y(k, 1),
    )

    def run(text):
        for action, which in zip(text[::2], text[1::2]):
            actions[action](int(which))

    for text in BEFORE:
        run(text)

    @pl.loop(0, 6)
    def _(i):
        for at, text in enumerate(STEPS):

            @pl.when(i == at)
            def _():
                run(text)

        half = jnp.where(i < 4, i // 2, i % 2)
        attend(jnp.where(i < 4, i % 2, 2), (half * 2, half * 2 + 1), False)

    run(AFTER)

    attend(3, range(NY), True)

    def done(ref, sem):
        pltpu.make_async_copy(ref, ref, sem).wait()

    done(stage.at[:, :, pl.ds(0, NZ * 2 * HD)], y_send.at[0])
    done(stage.at[:, :, pl.ds(0, NZ * HD)], y_send.at[1])
    done(qa.at[pl.ds(0, QUERIES - NY * ROWS), :], z_send.at[0])
    done(result.at[pl.ds(0, QUERIES - NY * ROWS), :], z_send.at[1])
    for i in range(8):
        ref = kv.at[:, :, 0, 0, pl.ds(0, LINE // 2), :] if i in (3, 4) else kv.at[:, :, 0, 0]
        done(ref, ring_send.at[i])
    done(result.at[pl.ds(0, QUERIES - ROWS), :], out_send.at[0])
    done(result, out_sem.at[0])


def on_device(tokens_qkv, block_mask):
    dma = pltpu.SemaphoreType.DMA
    return pl.pallas_call(
        kernel,
        out_shape=jax.ShapeDtypeStruct((ROWS, NY * NZ * HD), jnp.bfloat16),
        in_specs=[pl.BlockSpec(memory_space=pl.ANY), pl.BlockSpec(memory_space=pl.ANY)],
        out_specs=pl.BlockSpec(memory_space=pl.ANY),
        scratch_shapes=[
            pltpu.VMEM((ROWS, NY * NZ * 3 * HD), jnp.bfloat16),
            pltpu.VMEM((64, 64), jnp.int32),
            pltpu.VMEM((NY - 1, ROWS, NZ * 3 * HD), jnp.bfloat16),
            pltpu.VMEM((NY, 2, NX, NC, LINE, 2 * HD), jnp.bfloat16),
            pltpu.VMEM((QUERIES, 2 * HD), jnp.bfloat16),
            pltpu.VMEM((QUERIES, 2 * HD), jnp.float32),
            pltpu.VMEM((QUERIES, HD), jnp.float32),
            pltpu.VMEM((64, HD), jnp.float32),
            pltpu.VMEM((QUERIES, HD), jnp.bfloat16),
            dma((2,)),
            dma((NY - 1, 2)),
            dma((2,)),
            dma((NY,)),
            dma((NY, 2)),
            dma((2,)),
            dma((NY, 2, NX, NC)),
            dma((8,)),
            dma((1,)),
            dma((1,)),
        ],
        compiler_params=pltpu.CompilerParams(
            collective_id=0, has_side_effects=True, vmem_limit_bytes=62 * 1024 * 1024
        ),
        cost_estimate=pl.CostEstimate(flops=8 * 1024 * 8192 * 128, bytes_accessed=1 << 20, transcendentals=1024 * 8192),
    )(tokens_qkv, block_mask)


def solution(mesh):
    return jax.shard_map(
        on_device,
        mesh=mesh,
        in_specs=(P(("blk", "head"), None), P()),
        out_specs=P(("blk", "head"), None),
        check_vma=False,
    )
```

```python
import functools
import math

import jax
import jax.numpy as jnp
from jax import lax
from jax.experimental import pallas as pl
from jax.experimental.pallas import tpu as pltpu
from jax.sharding import PartitionSpec as P

MESH = pl.DeviceIdType.MESH
HD = 128
BLOCK = 128
ROWS = 32
NX, NY, NZ, NC = 4, 4, 8, 2
QUERIES = NY * NZ * ROWS
HALF = ROWS // 2
LINE = NZ * HALF
PIECE = 2 * NX * NC * LINE
TILE = 256
NEGATIVE = -1e30
EXPONENT = math.log2(math.e) / math.sqrt(HD)


BEFORE = (
    "Y1Y2K0Q0y1y2A0W1K1w1Q1W2K2Y3y3w2",
    "Q2W3K3w3Q3A1A2A3B0B1A4A5B2B3C0C1",
)
STEPS = ("A6S0R0R1", "A7B4B5C2C3S1", "B6R2R3", "B7C4C5", "C6S2", "C7")
AFTER = "S3"


def device_at(x, y, z, c):
    return ((z // 2) * NC + c, y * 8 + (z % 2) * NX + x)


def block_of(y, z, c):
    return ((z // 2) * NC + c) * 8 + y * 2 + z % 2


def aligned(start, size):
    return pl.ds(pl.multiple_of(start, size), size)


def kernel(
    tokens, mask, out, held, pairs, stage, kv, qa, acc, top, bias, result,
    in_sem, y_sem, y_send, q_sem, kv_sem, z_send, ring_sem, ring_send, out_sem, out_send,
):
    blk, place = lax.axis_index("blk"), lax.axis_index("head")
    c, y, x = blk % NC, place // 8, place % NX
    z = (blk // NC) * 2 + (place // NX) % 2
    head = y * NZ + z
    right, left, across = (x + 1) % NX, (x + NX - 1) % NX, (x + 2) % NX
    other = 1 - c
    source = (y, (y + 1) % NY, (y + NY - 1) % NY, (y + 2) % NY)
    at_y = (None, device_at(x, source[2], z, c), device_at(x, source[1], z, c), device_at(x, source[3], z, c))
    z_there = [(z + step) % NZ for step in (1, 7, 2, 6, 3, 5, 4)]
    at_z = [device_at(x, y, there, c) for there in z_there]
    at_right, at_left, at_other = device_at(right, y, z, c), device_at(left, y, z, c), device_at(x, y, z, other)

    load = pltpu.make_async_copy(tokens, held, in_sem.at[0])
    load.start()
    load_mask = pltpu.make_async_copy(mask, pairs, in_sem.at[1])
    load_mask.start()

    barrier = pltpu.get_barrier_semaphore()
    for where in [at_other, at_right, at_left] + list(at_y[1:]) + at_z:
        pl.semaphore_signal(barrier, inc=1, device_id=where, device_id_type=MESH)

    load_mask.wait()
    row_block = lax.broadcasted_iota(jnp.int32, (64, 64), 0)
    col_block = lax.broadcasted_iota(jnp.int32, (64, 64), 1)
    bias[...] = jnp.zeros_like(bias)
    bias[:, 0:64] = jnp.where((pairs[...] == 1) | (row_block == col_block), 0.0, NEGATIVE)

    @pl.loop(0, NY * NZ)
    def _(g):
        line = bias[pl.ds(block_of(g // NZ, g % NZ, c), 1), :]
        qa[aligned(g * ROWS, ROWS), HD : 2 * HD] = jnp.broadcast_to(line, (ROWS, HD)).astype(jnp.bfloat16)

    acc[...] = jnp.zeros_like(acc)
    top[...] = jnp.full_like(top, NEGATIVE)
    load.wait()
    pl.semaphore_wait(barrier, NY + NZ + 1)

    wide = NZ * 3 * HD

    def along_y(k, part):
        there = source[(0, 2, 1, 3)[k]]
        for i in range(NZ):
            start = (z_there[i] if i < NZ - 1 else z) * 3 * HD + (HD if part == 0 else 0)
            width = 2 * HD if part == 0 else HD
            pltpu.make_async_remote_copy(
                src_ref=held.at[:, pl.ds(pl.multiple_of(there * wide + start, HD), width)],
                dst_ref=stage.at[k - 1, :, pl.ds(pl.multiple_of(start, HD), width)],
                send_sem=y_send.at[part],
                recv_sem=y_sem.at[k - 1, part],
                device_id=at_y[k],
                device_id_type=MESH,
            ).start()

    def from_y(k, part):
        ref = stage.at[k - 1, :, pl.ds(0, NZ * (HD if part else 2 * HD))]
        pltpu.make_async_copy(ref, ref, y_sem.at[k - 1, part]).wait()

    def slab(k, there, part):
        width = HD if part == 2 else 2 * HD
        start = there * 3 * HD + (0 if part == 2 else HD)
        rows = pl.ds(0, ROWS) if part == 2 else pl.ds(part * HALF, HALF)
        if k == 0:
            return held.at[rows, pl.ds(pl.multiple_of(y * wide + start, HD), width)]
        return stage.at[k - 1, rows, pl.ds(pl.multiple_of(start, HD), width)]

    def landing(k, part):
        if part < 2:
            return kv.at[source[k], part, x, c, aligned(z * HALF, HALF), :]
        return qa.at[aligned((source[k] * NZ + z) * ROWS, ROWS), pl.ds(0, HD)]

    def along_z(k, part):
        sem = kv_sem.at[k, part] if part < 2 else q_sem.at[k]
        for i in range(NZ - 1):
            pltpu.make_async_remote_copy(
                src_ref=slab(k, z_there[i], part),
                dst_ref=landing(k, part),
                send_sem=z_send.at[part // 2],
                recv_sem=sem,
                device_id=at_z[i],
                device_id_type=MESH,
            ).start()
        pltpu.make_async_copy(slab(k, z, part), landing(k, part), sem).start()

    def ring(ref, sem, where, send):
        pltpu.make_async_remote_copy(
            src_ref=ref, dst_ref=ref, send_sem=ring_send.at[send], recv_sem=sem, device_id=where, device_id_type=MESH
        ).start()

    def pick(p):
        return lax.rem(y + (p + 1) // 2 * (2 * (p % 2) - 1) + NY, NY)

    def arrived(yp, h, xc, cc):
        ref = kv.at[yp, h, xc, cc]
        pltpu.make_async_copy(ref, ref, ring_sem.at[yp, h, xc, cc]).wait()

    def step_a(p):
        yp, h = source[p // 2], p % 2
        ref, sem = kv.at[yp, h, x, c], ring_sem.at[yp, h, x, c]
        pltpu.make_async_copy(ref, ref, kv_sem.at[p // 2, h]).wait()
        ring(ref, sem, at_right, 0)
        ring(ref, sem, at_left, 1)
        ring(ref, sem, at_other, 2)

    def step_b(p):
        yp, h = source[p // 2], p % 2
        for xc, half, onward, send in ((left, 0, at_right, 3), (right, 1, at_left, 4)):
            arrived(yp, h, xc, c)
            ring(kv.at[yp, h, xc, c, pl.ds(half * (LINE // 2), LINE // 2), :], ring_sem.at[yp, h, xc, c], onward, send)
        ring(kv.at[yp, h, left, c], ring_sem.at[yp, h, left, c], at_other, 5)
        ring(kv.at[yp, h, right, c], ring_sem.at[yp, h, right, c], at_other, 6)

    def step_c(p):
        yp, h = source[p // 2], p % 2
        arrived(yp, h, across, c)
        ring(kv.at[yp, h, across, c], ring_sem.at[yp, h, across, c], at_other, 7)

    def complete(k):
        for h in range(2):
            for xc in range(NX):
                arrived(source[k], h, xc, other)

    def send_tile(j):
        target = out.at[:, aligned(head * HD, HD)]

        @pl.loop(0, NZ)
        def _(pz):
            piece = result.at[aligned((j * NZ + pz) * ROWS, ROWS), :]
            mine = (j == y) & (pz == z)

            @pl.when(mine)
            def _():
                pltpu.make_async_copy(piece, target, out_sem.at[0]).start()

            @pl.when(jnp.logical_not(mine))
            def _():
                pltpu.make_async_remote_copy(
                    src_ref=piece, dst_ref=target, send_sem=out_send.at[0], recv_sem=out_sem.at[0],
                    device_id=device_at(x, j, pz, c), device_id_type=MESH,
                ).start()

    def attend(k, tiles, finish):
        yp = pick(k)
        row = lax.broadcasted_iota(jnp.int32, (NC * LINE, HD), 0)
        col = lax.broadcasted_iota(jnp.int32, (NC * LINE, HD), 1)
        hot = col == block_of(yp, (row // HALF) % NZ, row // LINE)
        hot = jnp.where(hot, 1.0, 0.0).astype(jnp.bfloat16)
        hot = jnp.concatenate([hot] * (2 * NX), axis=0)
        keys = jnp.concatenate([kv[yp, :, :, :, :, 0:HD].reshape(PIECE, HD), hot], axis=1)
        values = jnp.concatenate(
            [kv[yp, :, :, :, :, HD : 2 * HD].reshape(PIECE, HD), jnp.ones((PIECE, HD), jnp.bfloat16)], axis=1
        )

        def score(place):
            return lax.dot_general(
                qa[aligned(place * TILE, TILE), :], keys, (((1,), (1,)), ((), ())), preferred_element_type=jnp.float32
            )

        places = [pick(t) for t in tiles]
        ahead = score(places[0])
        for j, place in enumerate(places):
            rows = aligned(place * TILE, TILE)
            scores = ahead
            if j + 1 < len(places):
                ahead = score(places[j + 1])
            old = top[rows, :]
            new = jnp.maximum(old, jnp.max(scores, axis=1, keepdims=True))
            top[rows, :] = new
            weights = jnp.exp2(scores * EXPONENT - new[:, 0:1] * EXPONENT).astype(jnp.bfloat16)
            factor = jnp.exp2((old - new) * EXPONENT)
            total = acc[rows, :] * jnp.concatenate([factor, factor], axis=1) + jnp.dot(
                weights, values, preferred_element_type=jnp.float32
            )
            if finish:
                result[rows, :] = (total[:, 0:HD] / total[:, HD : 2 * HD]).astype(jnp.bfloat16)
                send_tile(place)
            else:
                acc[rows, :] = total

    def queries(k):
        ref = qa.at[aligned(source[k] * TILE, TILE), pl.ds(0, HD)]
        pltpu.make_async_copy(ref, ref, q_sem.at[k]).wait()

    def keys_of(k):
        along_z(k, 0)
        along_z(k, 1)

    actions = dict(

        A=step_a, B=step_b, C=step_c, K=keys_of, Q=lambda k: along_z(k, 2), S=complete, R=queries,
        Y=lambda k: along_y(k, 0), y=lambda k: along_y(k, 1), W=lambda k: from_y(k, 0), w=lambda k: from_y(k, 1),
    )

    def run(text):
        for action, which in zip(text[::2], text[1::2]):
            actions[action](int(which))

    for text in BEFORE:
        run(text)

    @pl.loop(0, 6)
    def _(i):
        for at, text in enumerate(STEPS):

            @pl.when(i == at)
            def _():
                run(text)

        half = jnp.where(i < 4, i // 2, i % 2)
        attend(jnp.where(i < 4, i % 2, 2), (half * 2, half * 2 + 1), False)

    run(AFTER)

    attend(3, range(NY), True)

    def done(ref, sem):
        pltpu.make_async_copy(ref, ref, sem).wait()

    done(stage.at[:, :, pl.ds(0, NZ * 2 * HD)], y_send.at[0])
    done(stage.at[:, :, pl.ds(0, NZ * HD)], y_send.at[1])
    done(qa.at[pl.ds(0, QUERIES - NY * ROWS), :], z_send.at[0])
    done(result.at[pl.ds(0, QUERIES - NY * ROWS), :], z_send.at[1])
    for i in range(8):
        ref = kv.at[:, :, 0, 0, pl.ds(0, LINE // 2), :] if i in (3, 4) else kv.at[:, :, 0, 0]
        done(ref, ring_send.at[i])
    done(result.at[pl.ds(0, QUERIES - ROWS), :], out_send.at[0])
    done(result, out_sem.at[0])


def on_device(tokens_qkv, block_mask):
    dma = pltpu.SemaphoreType.DMA
    return pl.pallas_call(
        kernel,
        out_shape=jax.ShapeDtypeStruct((ROWS, NY * NZ * HD), jnp.bfloat16),
        in_specs=[pl.BlockSpec(memory_space=pl.ANY), pl.BlockSpec(memory_space=pl.ANY)],
        out_specs=pl.BlockSpec(memory_space=pl.ANY),
        scratch_shapes=[
            pltpu.VMEM((ROWS, NY * NZ * 3 * HD), jnp.bfloat16),
            pltpu.VMEM((64, 64), jnp.int32),
            pltpu.VMEM((NY - 1, ROWS, NZ * 3 * HD), jnp.bfloat16),
            pltpu.VMEM((NY, 2, NX, NC, LINE, 2 * HD), jnp.bfloat16),
            pltpu.VMEM((QUERIES, 2 * HD), jnp.bfloat16),
            pltpu.VMEM((QUERIES, 2 * HD), jnp.float32),
            pltpu.VMEM((QUERIES, HD), jnp.float32),
            pltpu.VMEM((64, HD), jnp.float32),
            pltpu.VMEM((QUERIES, HD), jnp.bfloat16),
            dma((2,)),
            dma((NY - 1, 2)),
            dma((2,)),
            dma((NY,)),
            dma((NY, 2)),
            dma((2,)),
            dma((NY, 2, NX, NC)),
            dma((8,)),
            dma((1,)),
            dma((1,)),
        ],
        compiler_params=pltpu.CompilerParams(
            collective_id=0, has_side_effects=True, vmem_limit_bytes=62 * 1024 * 1024
        ),
        cost_estimate=pl.CostEstimate(flops=8 * 1024 * 8192 * 128, bytes_accessed=1 << 20, transcendentals=1024 * 8192),
    )(tokens_qkv, block_mask)


def solution(mesh):
    return jax.shard_map(
        on_device,
        mesh=mesh,
        in_specs=(P(("blk", "head"), None), P()),
        out_specs=P(("blk", "head"), None),
        check_vma=False,
    )
```
